32 devices in a mesh: rep: 4 (over y, x), fsdp: 8 (over z, core).
Axes of the slice: x: 2, y: 2, z: 4, core: 2. Of those that a mesh axis runs over, the one named last changes fastest.
Arguments:
- accumulated: bfloat16 [4, 1024, 14336], P('rep', 'fsdp'), may hold values from -48 to 48
- start_q: bfloat16 [32, 14336], replicated, may hold values from -6 to 6
- max_rms: float32 [1], replicated, as said below
Outputs:
- update: bfloat16 [1024, 14336], P('fsdp', 'rep')
- next_q: float32 [32, 14336], P(None, ('rep', 'fsdp'))
The draws below stay inside these ranges and needn't reach their ends.
Inputs may be any that keep to these rules, and one draw needn't show every extreme that they name: `max_rms`: a positive threshold.
All inputs are finite; a program needn't handle non-finite values.
Results may differ from the reference program's by a relative error of at most 0.0064.
Values may be sent and summed in bfloat16 or wider, within the bound.
A program may use at most 64 MiB of HBM per device.

```python
import math
import jax
import jax.numpy as jnp
from jax import lax

N = 14336
RANK = 32
M = 1024
REPLICAS = 4


def draw_max_rms(key, part):
    key = jax.random.fold_in(key, 7)
    level = 8.0 * math.sqrt(REPLICAS * RANK / M)
    factor = jax.random.uniform(key, (1,), jnp.float32, 0.3, 0.6)
    return (level * factor).astype(jnp.float32)


def block_levels(stream_key, extent, split, smallest, largest):
    gain = 1.0
    for axis_at, shards_of in split:
        heights = jax.random.uniform(jax.random.fold_in(jax.random.fold_in(stream_key, 6), axis_at), (shards_of,), jnp.float32, smallest / len(split), largest / len(split))
        gain = gain * jnp.repeat(jnp.exp(heights), extent[axis_at] // shards_of).reshape((-1,) + (1,) * (len(extent) - 1 - axis_at))
    return gain


def normal_values(stream_key, dims, width, reach, shards=(), kind=jnp.bfloat16):
    drawn = jax.random.normal(stream_key, dims, jnp.float32) * width
    if len(shards) > 0:
        drawn = block_levels(stream_key, dims, shards, -0.22, 0.18) * drawn
    return jnp.clip(drawn, min=-reach, max=reach).astype(kind)


def setup_inputs(seed: int = 0) -> dict:
    key_list = jax.random.split(jax.random.key(seed), 4)
    accumulated = normal_values(key_list[0], (REPLICAS, M, N), 8.0, 48.0, ((0, 4), (1, 8)))
    start_q = normal_values(key_list[1], (RANK, N), 1.0, 6.0)
    max_rms = draw_max_rms(jax.random.fold_in(key_list[3], 71), 0)
    return {"accumulated": accumulated, "start_q": start_q, "max_rms": max_rms}


def reference(accumulated, start_q, max_rms):

    def p_term(total, grad):
        term = lax.dot_general(grad.astype(jnp.float32), start_q.astype(jnp.float32), (((1,), (1,)), ((), ())), preferred_element_type=jnp.float32)
        return (total + term, None)
    p_sum, _ = lax.scan(p_term, jnp.zeros((M, RANK), jnp.float32), accumulated)
    gram = jnp.dot(p_sum.T, p_sum, precision=lax.Precision.HIGHEST)
    lower = jnp.linalg.cholesky(gram)
    p_hat = lax.linalg.triangular_solve(lower, p_sum, left_side=False, lower=True, transpose_a=True)
    p_round = p_hat.astype(jnp.bfloat16)

    def q_term(total, grad):
        term = lax.dot_general(p_round.astype(jnp.float32), grad.astype(jnp.float32), (((0,), (0,)), ((), ())), preferred_element_type=jnp.float32)
        return (total + term, None)
    next_q, _ = lax.scan(q_term, jnp.zeros((RANK, N), jnp.float32), accumulated)
    norm = jnp.sqrt(jnp.sum(next_q * next_q))
    scale = jnp.minimum(1.0, max_rms[0] * math.sqrt(M * N) / norm)
    q_round = next_q.astype(jnp.bfloat16)
    update = (scale * jnp.dot(p_round.astype(jnp.float32), q_round.astype(jnp.float32), preferred_element_type=jnp.float32)).astype(jnp.bfloat16)
    return (update, next_q)
```

```python
import math

import jax
import jax.numpy as jnp
from jax import lax
from jax.experimental import pallas as pl
from jax.experimental.pallas import tpu as pltpu
from jax.sharding import PartitionSpec as P


MESH = pl.DeviceIdType.MESH
F32 = jnp.float32
BF16 = jnp.bfloat16
REPS = 4
FSDP = 8
CHIPS = 4
RANK = 32
HALF = 16
FLIPS = ((1, 1), (0, 1), (1, 0), (0, 0))


def round_kernel(
    acc_hbm, startq_hbm, max_rms, update_ref, nextq_ref,
    shard, startq, p_all, g_all, own_q, core_out, core_in, rep_out, rep_in,
    total, z_out, z_in, gathered, final, final_in, norms, product,
    load_sem, loadq_sem, p_send, p_recv, g_send, g_recv, core_send, core_recv,
    rep_send, rep_recv, z_send, z_recv, ag_send, ag_recv, relay_send, relay_recv,
    fin_send, fin_recv, norm_send, norm_recv,
):
    rep = lax.axis_index("rep")
    fsdp = lax.axis_index("fsdp")
    z, core = fsdp // 2, fsdp % 2
    y, x = rep // 2, rep % 2
    block = shard.shape[2]
    piece = block // CHIPS
    elements = shard.shape[1] * FSDP * block * REPS
    reps = [((y + dy) % 2) * 2 + (x + dx) % 2 for dy, dx in FLIPS]
    partner = z * 2 + (core + 1) % 2

    def remote(src, dst, send, recv, to_rep, to_fsdp):
        copy = pltpu.make_async_remote_copy(
            src_ref=src, dst_ref=dst, send_sem=send, recv_sem=recv,
            device_id=(to_rep, to_fsdp), device_id_type=MESH,
        )
        copy.start()
        return copy

    loads = []
    for c in range(REPS):
        columns = pl.ds(c * block, block)
        first = pltpu.make_async_copy(startq_hbm.at[:, columns], startq.at[c], loadq_sem.at[c])
        second = pltpu.make_async_copy(acc_hbm.at[0, :, columns], shard.at[c], load_sem.at[c])
        first.start()
        second.start()
        loads.append((first, second))

    barrier = pltpu.get_barrier_semaphore()
    for s in range(REPS - 1):
        pl.semaphore_signal(barrier, inc=1, device_id=(reps[s], fsdp), device_id_type=MESH)
    for d in range(1, FSDP):
        pl.semaphore_signal(
            barrier, inc=1, device_id=(rep, (fsdp + d) % FSDP), device_id_type=MESH
        )

    local_p = jnp.zeros((RANK, shard.shape[1]), F32)
    for c in range(REPS):
        for load in loads[c]:
            load.wait()
        local_p += lax.dot_general(
            startq[c], shard[c], (((1,), (1,)), ((), ())), preferred_element_type=F32
        )
    p_all[rep] = local_p
    pl.semaphore_wait(barrier, REPS - 1 + FSDP - 1)

    copies = [
        remote(p_all.at[rep], p_all.at[rep], p_send.at[s], p_recv.at[s], reps[s], fsdp)
        for s in range(REPS - 1)
    ]
    for copy in copies:
        copy.wait_recv()
    p_sum = p_all[0] + p_all[1] + p_all[2] + p_all[3]
    padded = jnp.concatenate([p_sum, jnp.zeros((128 - RANK, p_sum.shape[1]), F32)], axis=0)
    g_all[fsdp] = lax.dot_general(
        p_sum, padded, (((1,), (1,)), ((), ())),
        precision=lax.Precision.HIGHEST, preferred_element_type=F32,
    )
    sends = list(copies)
    copies = [
        remote(
            g_all.at[fsdp], g_all.at[fsdp], g_send.at[d - 1], g_recv.at[d - 1],
            rep, (fsdp + d) % FSDP,
        )
        for d in range(1, FSDP)
    ]
    for copy in copies:
        copy.wait_recv()
    sends += copies
    gram = g_all[0]
    for i in range(1, FSDP):
        gram = gram + g_all[i]

    g = [gram[8 * t : 8 * t + 8] for t in range(RANK // 8)]
    p = [p_sum[8 * t : 8 * t + 8] for t in range(RANK // 8)]
    line = lax.broadcasted_iota(jnp.int32, (8, 128), 0)
    pivots = [jnp.ones((8, 128), F32) for _ in g]
    for k in range(RANK):
        t, r = k // 8, k % 8
        row_g, row_p = g[t][r : r + 1], p[t][r : r + 1]
        pivot = row_g[:, k : k + 1]
        pivots[t] = jnp.where(line == r, pivot, pivots[t])
        inverse = 1.0 / pivot
        row_g, row_p = row_g * inverse, row_p * inverse
        for u in range(t, RANK // 8):
            factor = jnp.broadcast_to(g[u][:, k : k + 1], (8, 128))
            if u == t:
                factor = jnp.where(line > r, factor, 0.0)
            g[u] = g[u] - factor * row_g
            p[u] = p[u] - factor * row_p
    p_hat = [p[t] * lax.rsqrt(pivots[t]) for t in range(RANK // 8)]
    p_round = jnp.concatenate(p_hat, axis=0).astype(BF16)
    lower_half = jnp.concatenate(p_hat[:2], axis=0)
    upper_half = jnp.concatenate(p_hat[2:], axis=0)
    is_first = core == 0
    own_first = jnp.concatenate(
        [jnp.where(is_first, lower_half, upper_half), jnp.where(is_first, upper_half, lower_half)],
        axis=0,
    ).astype(BF16)

    core_copies, rep_copies = [], []

    def to_replica(s):
        core_copies[s].wait_recv()
        summed = own_q[s] + core_in[s].astype(F32)
        if s < REPS - 1:
            rep_out[s] = summed.astype(BF16)
            rep_copies.append(
                remote(
                    rep_out.at[s], rep_in.at[s], rep_send.at[s], rep_recv.at[s], reps[s], fsdp
                )
            )
        else:
            own_q[s] = summed

    for s in range(REPS):
        terms = jnp.dot(own_first, shard[reps[s]], preferred_element_type=F32)
        own_q[s] = terms[:HALF]
        core_out[s] = terms[HALF:].astype(BF16)
        core_copies.append(
            remote(
                core_out.at[s], core_in.at[s], core_send.at[s], core_recv.at[s], rep, partner
            )
        )
        if s > 0:
            to_replica(s - 1)
    to_replica(REPS - 1)
    sends += core_copies + rep_copies

    for copy in rep_copies:
        copy.wait_recv()
    for q in range(CHIPS):
        columns = pl.ds(q * piece, piece)
        value = own_q[REPS - 1, :, columns]
        for s in range(REPS - 1):
            value = value + rep_in[s, :, columns].astype(F32)
        total[q] = value
    z_copies = []
    for d in (2, 1, 3):
        to = (z + d) % CHIPS
        z_out[d - 1] = total[to].astype(BF16)
        z_copies.append(
            remote(
                z_out.at[d - 1], z_in.at[d - 1], z_send.at[d - 1], z_recv.at[d - 1],
                rep, to * 2 + core,
            )
        )
    for copy in z_copies:
        copy.wait_recv()
    sends += z_copies
    mine = total[z] + z_in[0].astype(F32) + z_in[1].astype(F32) + z_in[2].astype(F32)
    final[...] = mine
    gathered[core, z] = mine.astype(BF16)
    ag_copies = []
    for d in (2, 1, 3):
        ag_copies.append(
            remote(
                gathered.at[core, z], gathered.at[core, z], ag_send.at[d - 1],
                ag_recv.at[d - 1], rep, ((z + d) % CHIPS) * 2 + core,
            )
        )
    relays = [
        remote(
            gathered.at[core, z], gathered.at[core, z], relay_send.at[0], relay_recv.at[0],
            rep, partner,
        )
    ]
    fin_copy = remote(final, final_in, fin_send, fin_recv, rep, partner)
    for copy, d in zip(ag_copies, (2, 1, 3)):
        copy.wait_recv()
        source = (z + CHIPS - d) % CHIPS
        relays.append(
            remote(
                gathered.at[core, source], gathered.at[core, source], relay_send.at[d],
                relay_recv.at[d], rep, partner,
            )
        )
    nextq_ref[pl.ds(pl.multiple_of(core * HALF, HALF), HALF), :] = mine
    fin_copy.wait_recv()
    nextq_ref[pl.ds(pl.multiple_of((1 - core) * HALF, HALF), HALF), :] = final_in[...]
    for copy in relays:
        copy.wait_recv()
    sends += ag_copies + relays + [fin_copy]

    squares = jnp.zeros((1, piece), F32)
    for q in range(CHIPS):
        for h in range(2):
            value = gathered[h, q].astype(F32)
            squares = squares + jnp.sum(value * value, axis=0, keepdims=True)
    norms[rep] = jnp.broadcast_to(jnp.sum(squares, axis=1, keepdims=True), (8, 128))
    copies = [
        remote(norms.at[rep], norms.at[rep], norm_send.at[s], norm_recv.at[s], reps[s], fsdp)
        for s in range(REPS - 1)
    ]
    sends += copies
    for q in range(CHIPS):
        right = jnp.concatenate([gathered[0, q], gathered[1, q]], axis=0)
        product[q] = lax.dot_general(
            p_round, right, (((0,), (0,)), ((), ())), preferred_element_type=F32
        )
    for copy in copies:
        copy.wait_recv()
    norm_sq = (norms[0] + norms[1] + norms[2] + norms[3])[:1, :1]
    limit = max_rms[0] * math.sqrt(elements)
    scale = jnp.minimum(1.0, limit / jnp.sqrt(norm_sq))
    for q in range(CHIPS):
        update_ref[:, pl.ds(q * piece, piece)] = (scale * product[q]).astype(BF16)
    for copy in sends:
        copy.wait_send()


def on_block(accumulated, start_q, max_rms):
    rows, width = accumulated.shape[1:]
    block = width // REPS
    piece = block // CHIPS
    dma = pltpu.SemaphoreType.DMA
    update, chip_q = pl.pallas_call(
        round_kernel,
        out_shape=(
            jax.ShapeDtypeStruct((rows, block), BF16),
            jax.ShapeDtypeStruct((RANK, piece), F32),
        ),
        in_specs=[
            pl.BlockSpec(memory_space=pl.ANY),
            pl.BlockSpec(memory_space=pl.ANY),
            pl.BlockSpec(memory_space=pltpu.SMEM),
        ],
        out_specs=(
            pl.BlockSpec(memory_space=pltpu.VMEM),
            pl.BlockSpec(memory_space=pltpu.VMEM),
        ),
        scratch_shapes=[
            pltpu.VMEM((REPS, rows, block), BF16),
            pltpu.VMEM((REPS, RANK, block), BF16),
            pltpu.VMEM((REPS, RANK, rows), F32),
            pltpu.VMEM((FSDP, RANK, 128), F32),
            pltpu.VMEM((REPS, HALF, block), F32),
            pltpu.VMEM((REPS, HALF, block), BF16),
            pltpu.VMEM((REPS, HALF, block), BF16),
            pltpu.VMEM((REPS - 1, HALF, block), BF16),
            pltpu.VMEM((REPS - 1, HALF, block), BF16),
            pltpu.VMEM((CHIPS, HALF, piece), F32),
            pltpu.VMEM((CHIPS - 1, HALF, piece), BF16),
            pltpu.VMEM((CHIPS - 1, HALF, piece), BF16),
            pltpu.VMEM((2, CHIPS, HALF, piece), BF16),
            pltpu.VMEM((HALF, piece), F32),
            pltpu.VMEM((HALF, piece), F32),
            pltpu.VMEM((REPS, 8, 128), F32),
            pltpu.VMEM((CHIPS, rows, piece), F32),
            dma((REPS,)), dma((REPS,)),
            dma((REPS - 1,)), dma((REPS - 1,)),
            dma((FSDP - 1,)), dma((FSDP - 1,)),
            dma((REPS,)), dma((REPS,)),
            dma((REPS - 1,)), dma((REPS - 1,)),
            dma((CHIPS - 1,)), dma((CHIPS - 1,)),
            dma((CHIPS - 1,)), dma((CHIPS - 1,)),
            dma((CHIPS,)), dma((CHIPS,)),
            dma, dma,
            dma((REPS - 1,)), dma((REPS - 1,)),
        ],
        compiler_params=pltpu.CompilerParams(
            collective_id=0, has_side_effects=True, vmem_limit_bytes=40 * 1024 * 1024
        ),
    )(accumulated, start_q, max_rms)
    own = piece // 2
    next_q = lax.dynamic_slice_in_dim(chip_q, (lax.axis_index("fsdp") % 2) * own, own, 1)
    return (update, next_q)


def orthonormal(part_rows, gram):
    lower = jnp.linalg.cholesky(gram)
    return lax.linalg.triangular_solve(
        lower, part_rows, left_side=False, lower=True, transpose_a=True
    )


def on_device(accumulated, start_q, max_rms):
    shard = accumulated[0]
    rows = shard.shape[0]
    width = shard.shape[1]
    n_rep = lax.axis_size("rep")
    n_fsdp = lax.axis_size("fsdp")
    total_rows = rows * n_fsdp
    local_p = lax.dot_general(
        shard, start_q, (((1,), (1,)), ((), ())), preferred_element_type=jnp.float32
    )
    p_sum = lax.psum(local_p, "rep")
    gram = lax.psum(jnp.dot(p_sum.T, p_sum, precision=lax.Precision.HIGHEST), "fsdp")
    p_round = orthonormal(p_sum, gram).astype(jnp.bfloat16)
    block_cols = width // n_rep
    own_cols = width // (n_rep * n_fsdp)
    q_full = lax.psum(
        lax.dot_general(
            p_round, shard, (((0,), (0,)), ((), ())), preferred_element_type=jnp.float32
        ),
        ("rep", "fsdp"),
    )
    norm_sq = jnp.sum(q_full * q_full)
    q_block = lax.dynamic_slice_in_dim(
        q_full, lax.axis_index("rep") * block_cols, block_cols, 1
    ).astype(jnp.bfloat16)
    product = jnp.dot(p_round, q_block, preferred_element_type=jnp.float32)
    next_q = lax.dynamic_slice_in_dim(
        q_full, lax.axis_index(("rep", "fsdp")) * own_cols, own_cols, 1
    )
    scale = jnp.minimum(1.0, max_rms[0] * math.sqrt(total_rows * width) / jnp.sqrt(norm_sq))
    update = (scale * product).astype(jnp.bfloat16)
    return (update, next_q)


def solution(mesh):
    fits = mesh.shape["rep"] == REPS and mesh.shape["fsdp"] == FSDP
    return jax.shard_map(
        on_block if fits else on_device,
        mesh=mesh,
        in_specs=(P("rep", "fsdp", None), P(), P()),
        out_specs=(P("fsdp", "rep"), P(None, ("rep", "fsdp"))),
        check_vma=False,
    )
```

```python
import math

import jax
import jax.numpy as jnp
from jax import lax
from jax.experimental import pallas as pl
from jax.experimental.pallas import tpu as pltpu
from jax.sharding import PartitionSpec as P


MESH = pl.DeviceIdType.MESH
F32 = jnp.float32
BF16 = jnp.bfloat16
REPS = 4
FSDP = 8
CHIPS = 4
RANK = 32
HALF = 16
AWAY = (2, 1, 3)
LAG = 4
FLIPS = ((1, 1), (0, 1), (1, 0), (0, 0))


def round_kernel(
    acc_hbm, startq_hbm, max_rms, update_ref, nextq_ref,
    shard, startq, p_all, g_all, own_q, core_out, core_in, rep_out, rep_in,
    total, z_out, z_in, gathered, final, final_in, norms, all_norms,
    load_sem, loadq_sem, p_send, p_recv, g_send, g_recv, core_send, core_recv,
    rep_send, rep_recv, z_send, z_recv, ag_send, ag_recv, relay_send, relay_recv,
    fin_send, fin_recv, norm_send, norm_recv, all_send, all_recv,
):
    rep = lax.axis_index("rep")
    fsdp = lax.axis_index("fsdp")
    z, core = fsdp // 2, fsdp % 2
    y, x = rep // 2, rep % 2
    block = shard.shape[2]
    piece = block // CHIPS
    elements = shard.shape[1] * FSDP * block * REPS
    reps = [((y + dy) % 2) * 2 + (x + dx) % 2 for dy, dx in FLIPS]
    partner = z * 2 + (core + 1) % 2

    def remote(src, dst, send, recv, to_rep, to_fsdp):
        copy = pltpu.make_async_remote_copy(
            src_ref=src, dst_ref=dst, send_sem=send, recv_sem=recv,
            device_id=(to_rep, to_fsdp), device_id_type=MESH,
        )
        copy.start()
        return copy

    loads = []
    for c in range(REPS):
        columns = pl.ds(c * block, block)
        first = pltpu.make_async_copy(startq_hbm.at[:, columns], startq.at[c], loadq_sem.at[c])
        second = pltpu.make_async_copy(acc_hbm.at[0, :, columns], shard.at[c], load_sem.at[c])
        first.start()
        second.start()
        loads.append((first, second))

    barrier = pltpu.get_barrier_semaphore()
    for s in range(REPS - 1):
        pl.semaphore_signal(barrier, inc=1, device_id=(reps[s], fsdp), device_id_type=MESH)
    for d in range(1, FSDP):
        pl.semaphore_signal(
            barrier, inc=1, device_id=(rep, (fsdp + d) % FSDP), device_id_type=MESH
        )

    local_p = jnp.zeros((RANK, shard.shape[1]), F32)
    for c in range(REPS):
        for load in loads[c]:
            load.wait()
        local_p += lax.dot_general(
            startq[c], shard[c], (((1,), (1,)), ((), ())), preferred_element_type=F32
        )
    p_all[rep] = local_p
    pl.semaphore_wait(barrier, REPS - 1 + FSDP - 1)
    sends = []

    copies = [
        remote(p_all.at[rep], p_all.at[rep], p_send.at[s], p_recv.at[s], reps[s], fsdp)
        for s in range(REPS - 1)
    ]
    for copy in copies:
        copy.wait_recv()
    p_sum = p_all[0] + p_all[1] + p_all[2] + p_all[3]
    padded = jnp.concatenate([p_sum, jnp.zeros((128 - RANK, p_sum.shape[1]), F32)], axis=0)
    g_all[fsdp] = lax.dot_general(
        p_sum, padded, (((1,), (1,)), ((), ())),
        precision=lax.Precision.HIGHEST, preferred_element_type=F32,
    )
    sends += copies
    copies = [
        remote(
            g_all.at[fsdp], g_all.at[fsdp], g_send.at[d - 1], g_recv.at[d - 1],
            rep, (fsdp + d) % FSDP,
        )
        for d in range(1, FSDP)
    ]
    for copy in copies:
        copy.wait_recv()
    sends += copies
    gram = g_all[0]
    for i in range(1, FSDP):
        gram = gram + g_all[i]

    g = [gram[8 * t : 8 * t + 8] for t in range(RANK // 8)]
    p = [p_sum[8 * t : 8 * t + 8] for t in range(RANK // 8)]
    line = lax.broadcasted_iota(jnp.int32, (8, 128), 0)
    pivots = [jnp.ones((8, 128), F32) for _ in g]
    for k in range(RANK):
        t, r = k // 8, k % 8
        row_g, row_p = g[t][r : r + 1], p[t][r : r + 1]
        pivot = row_g[:, k : k + 1]
        pivots[t] = jnp.where(line == r, pivot, pivots[t])
        inverse = 1.0 / pivot
        row_g, row_p = row_g * inverse, row_p * inverse
        for u in range(t, RANK // 8):
            factor = jnp.broadcast_to(g[u][:, k : k + 1], (8, 128))
            if u == t:
                factor = jnp.where(line > r, factor, 0.0)
            g[u] = g[u] - factor * row_g
            p[u] = p[u] - factor * row_p
    p_hat = [p[t] * lax.rsqrt(pivots[t]) for t in range(RANK // 8)]
    p_round = jnp.concatenate(p_hat, axis=0).astype(BF16)
    lower_half = jnp.concatenate(p_hat[:2], axis=0)
    upper_half = jnp.concatenate(p_hat[2:], axis=0)
    is_first = core == 0
    own_first = jnp.concatenate(
        [jnp.where(is_first, lower_half, upper_half), jnp.where(is_first, upper_half, lower_half)],
        axis=0,
    ).astype(BF16)

    quarters = [(z + d) % CHIPS for d in AWAY + (0,)]
    pieces = [(i, s) for i in range(CHIPS) for s in range(REPS - 1)]
    pieces += [(i, REPS - 1) for i in range(CHIPS)]
    core_copies, rep_copies = [], {}

    def to_replica(n):
        i, s = pieces[n]
        core_copies[n].wait_recv()
        summed = own_q[n] + core_in[n].astype(F32)
        if s < REPS - 1:
            rep_out[n] = summed.astype(BF16)
            rep_copies[i, s] = remote(
                rep_out.at[n], rep_in.at[n], rep_send.at[n], rep_recv.at[n], reps[s], fsdp
            )
        else:
            total[i] = summed

    for n, (i, s) in enumerate(pieces):
        columns = pl.ds(pl.multiple_of(quarters[i] * piece, 128), piece)
        terms = jnp.dot(own_first, shard[reps[s], :, columns], preferred_element_type=F32)
        own_q[n] = terms[:HALF]
        core_out[n] = terms[HALF:].astype(BF16)
        core_copies.append(
            remote(
                core_out.at[n], core_in.at[n], core_send.at[n], core_recv.at[n], rep, partner
            )
        )
        if n >= LAG:
            to_replica(n - LAG)
    for n in range(len(pieces) - LAG, len(pieces)):
        to_replica(n)
    sends += core_copies + list(rep_copies.values())

    z_copies = []
    for i in range(CHIPS):
        value = total[i]
        for s in range(REPS - 1):
            rep_copies[i, s].wait_recv()
            value = value + rep_in[pieces.index((i, s))].astype(F32)
        if i < CHIPS - 1:
            z_out[i] = value.astype(BF16)
            z_copies.append(
                remote(
                    z_out.at[i], z_in.at[i], z_send.at[i], z_recv.at[i],
                    rep, quarters[i] * 2 + core,
                )
            )
        else:
            mine = value
    sends += z_copies
    for copy, i in zip(z_copies, range(CHIPS - 1)):
        copy.wait_recv()
        mine = mine + z_in[i].astype(F32)
    final[...] = mine
    gathered[core, z] = mine.astype(BF16)
    ag_copies = [
        remote(
            gathered.at[core, z], gathered.at[core, z], ag_send.at[i], ag_recv.at[i],
            rep, quarters[i] * 2 + core,
        )
        for i in range(CHIPS - 1)
    ]
    relays = [
        remote(
            gathered.at[core, z], gathered.at[core, z], relay_send.at[CHIPS - 1],
            relay_recv.at[CHIPS - 1], rep, partner,
        )
    ]
    fin_copy = remote(final, final_in, fin_send, fin_recv, rep, partner)
    squares = jnp.sum(jnp.sum(mine * mine, axis=0, keepdims=True), axis=1, keepdims=True)
    norms[rep] = jnp.broadcast_to(squares, (8, 128))
    norm_copies = [
        remote(norms.at[rep], norms.at[rep], norm_send.at[s], norm_recv.at[s], reps[s], fsdp)
        for s in range(REPS - 1)
    ]
    nextq_ref[pl.ds(pl.multiple_of(core * HALF, HALF), HALF), :] = mine
    for copy in norm_copies:
        copy.wait_recv()
    all_norms[fsdp] = norms[0] + norms[1] + norms[2] + norms[3]
    all_copies = [
        remote(
            all_norms.at[fsdp], all_norms.at[fsdp], all_send.at[d - 1], all_recv.at[d - 1],
            rep, (fsdp + d) % FSDP,
        )
        for d in range(1, FSDP)
    ]
    sources = [(z + CHIPS - d) % CHIPS for d in AWAY] + [z]
    for i in range(CHIPS - 1):
        ag_copies[i].wait_recv()
        relays.append(
            remote(
                gathered.at[core, sources[i]], gathered.at[core, sources[i]],
                relay_send.at[i], relay_recv.at[i], rep, partner,
            )
        )
    fin_copy.wait_recv()
    nextq_ref[pl.ds(pl.multiple_of((1 - core) * HALF, HALF), HALF), :] = final_in[...]
    for copy in all_copies:
        copy.wait_recv()
    norm_sq = all_norms[0]
    for i in range(1, FSDP):
        norm_sq = norm_sq + all_norms[i]
    sends += ag_copies + relays + [fin_copy] + norm_copies + all_copies
    limit = max_rms[0] * math.sqrt(elements)
    scale = jnp.minimum(1.0, limit / jnp.sqrt(norm_sq[:1, :1]))
    for copy, q in zip(relays, sources[-1:] + sources[:-1]):
        copy.wait_recv()
        right = jnp.concatenate([gathered[0, q], gathered[1, q]], axis=0)
        product = lax.dot_general(
            p_round, right, (((0,), (0,)), ((), ())), preferred_element_type=F32
        )
        columns = pl.ds(pl.multiple_of(q * piece, 128), piece)
        update_ref[:, columns] = (scale * product).astype(BF16)
    for copy in sends:
        copy.wait_send()


def on_block(accumulated, start_q, max_rms):
    rows, width = accumulated.shape[1:]
    block = width // REPS
    piece = block // CHIPS
    dma = pltpu.SemaphoreType.DMA
    update, chip_q = pl.pallas_call(
        round_kernel,
        out_shape=(
            jax.ShapeDtypeStruct((rows, block), BF16),
            jax.ShapeDtypeStruct((RANK, piece), F32),
        ),
        in_specs=[
            pl.BlockSpec(memory_space=pltpu.HBM),
            pl.BlockSpec(memory_space=pltpu.HBM),
            pl.BlockSpec(memory_space=pltpu.SMEM),
        ],
        out_specs=(
            pl.BlockSpec(memory_space=pltpu.VMEM),
            pl.BlockSpec(memory_space=pltpu.VMEM),
        ),
        scratch_shapes=[
            pltpu.VMEM((REPS, rows, block), BF16),
            pltpu.VMEM((REPS, RANK, block), BF16),
            pltpu.VMEM((REPS, RANK, rows), F32),
            pltpu.VMEM((FSDP, RANK, 128), F32),
            pltpu.VMEM((REPS * CHIPS, HALF, piece), F32),
            pltpu.VMEM((REPS * CHIPS, HALF, piece), BF16),
            pltpu.VMEM((REPS * CHIPS, HALF, piece), BF16),
            pltpu.VMEM(((REPS - 1) * CHIPS, HALF, piece), BF16),
            pltpu.VMEM(((REPS - 1) * CHIPS, HALF, piece), BF16),
            pltpu.VMEM((CHIPS, HALF, piece), F32),
            pltpu.VMEM((CHIPS - 1, HALF, piece), BF16),
            pltpu.VMEM((CHIPS - 1, HALF, piece), BF16),
            pltpu.VMEM((2, CHIPS, HALF, piece), BF16),
            pltpu.VMEM((HALF, piece), F32),
            pltpu.VMEM((HALF, piece), F32),
            pltpu.VMEM((REPS, 8, 128), F32),
            pltpu.VMEM((FSDP, 8, 128), F32),
            dma((REPS,)), dma((REPS,)),
            dma((REPS - 1,)), dma((REPS - 1,)),
            dma((FSDP - 1,)), dma((FSDP - 1,)),
            dma((REPS * CHIPS,)), dma((REPS * CHIPS,)),
            dma(((REPS - 1) * CHIPS,)), dma(((REPS - 1) * CHIPS,)),
            dma((CHIPS - 1,)), dma((CHIPS - 1,)),
            dma((CHIPS - 1,)), dma((CHIPS - 1,)),
            dma((CHIPS,)), dma((CHIPS,)),
            dma, dma,
            dma((REPS - 1,)), dma((REPS - 1,)),
            dma((FSDP - 1,)), dma((FSDP - 1,)),
        ],
        compiler_params=pltpu.CompilerParams(
            collective_id=0, has_side_effects=True, vmem_limit_bytes=40 * 1024 * 1024
        ),
    )(accumulated, start_q, max_rms)
    own = piece // 2
    next_q = lax.dynamic_slice_in_dim(chip_q, (lax.axis_index("fsdp") % 2) * own, own, 1)
    return (update, next_q)


def orthonormal(part_rows, gram):
    lower = jnp.linalg.cholesky(gram)
    return lax.linalg.triangular_solve(
        lower, part_rows, left_side=False, lower=True, transpose_a=True
    )


def on_device(accumulated, start_q, max_rms):
    shard = accumulated[0]
    rows = shard.shape[0]
    width = shard.shape[1]
    n_rep = lax.axis_size("rep")
    n_fsdp = lax.axis_size("fsdp")
    total_rows = rows * n_fsdp
    local_p = lax.dot_general(
        shard, start_q, (((1,), (1,)), ((), ())), preferred_element_type=jnp.float32
    )
    p_sum = lax.psum(local_p, "rep")
    gram = lax.psum(jnp.dot(p_sum.T, p_sum, precision=lax.Precision.HIGHEST), "fsdp")
    p_round = orthonormal(p_sum, gram).astype(jnp.bfloat16)
    block_cols = width // n_rep
    own_cols = width // (n_rep * n_fsdp)
    q_full = lax.psum(
        lax.dot_general(
            p_round, shard, (((0,), (0,)), ((), ())), preferred_element_type=jnp.float32
        ),
        ("rep", "fsdp"),
    )
    norm_sq = jnp.sum(q_full * q_full)
    q_block = lax.dynamic_slice_in_dim(
        q_full, lax.axis_index("rep") * block_cols, block_cols, 1
    ).astype(jnp.bfloat16)
    product = jnp.dot(p_round, q_block, preferred_element_type=jnp.float32)
    next_q = lax.dynamic_slice_in_dim(
        q_full, lax.axis_index(("rep", "fsdp")) * own_cols, own_cols, 1
    )
    scale = jnp.minimum(1.0, max_rms[0] * math.sqrt(total_rows * width) / jnp.sqrt(norm_sq))
    update = (scale * product).astype(jnp.bfloat16)
    return (update, next_q)


def solution(mesh):
    fits = mesh.shape["rep"] == REPS and mesh.shape["fsdp"] == FSDP
    return jax.shard_map(
        on_block if fits else on_device,
        mesh=mesh,
        in_specs=(P("rep", "fsdp", None), P(), P()),
        out_specs=(P("fsdp", "rep"), P(None, ("rep", "fsdp"))),
        check_vma=False,
    )
```

```python
import math

import jax
import jax.numpy as jnp
from jax import lax
from jax.experimental import pallas as pl
from jax.experimental.pallas import tpu as pltpu
from jax.sharding import PartitionSpec as P


MESH = pl.DeviceIdType.MESH
F32 = jnp.float32
BF16 = jnp.bfloat16
REPS = 4
FSDP = 8
CHIPS = 4
RANK = 32
HALF = 16
AWAY = (2, 1, 3)
LAG = 4
FLIPS = ((1, 1), (0, 1), (1, 0), (0, 0))


def round_kernel(
    acc_hbm, startq_hbm, max_rms, update_ref, nextq_ref,
    shard, startq, p_all, g_all, own_q, core_out, core_in, rep_out, rep_in,
    total, z_out, z_in, gathered, final, final_in, norms, all_norms, products,
    load_sem, loadq_sem, p_send, p_recv, g_send, g_recv, core_send, core_recv,
    rep_send, rep_recv, z_send, z_recv, ag_send, ag_recv, relay_send, relay_recv,
    fin_send, fin_recv, norm_send, norm_recv, all_send, all_recv,
):
    rep = lax.axis_index("rep")
    fsdp = lax.axis_index("fsdp")
    z, core = fsdp // 2, fsdp % 2
    y, x = rep // 2, rep % 2
    block = shard.shape[2]
    piece = block // CHIPS
    elements = shard.shape[1] * FSDP * block * REPS
    reps = [((y + dy) % 2) * 2 + (x + dx) % 2 for dy, dx in FLIPS]
    partner = z * 2 + (core + 1) % 2

    def remote(src, dst, send, recv, to_rep, to_fsdp):
        copy = pltpu.make_async_remote_copy(
            src_ref=src, dst_ref=dst, send_sem=send, recv_sem=recv,
            device_id=(to_rep, to_fsdp), device_id_type=MESH,
        )
        copy.start()
        return copy

    loads = []
    for c in range(REPS):
        columns = pl.ds(c * block, block)
        first = pltpu.make_async_copy(startq_hbm.at[:, columns], startq.at[c], loadq_sem.at[c])
        second = pltpu.make_async_copy(acc_hbm.at[0, :, columns], shard.at[c], load_sem.at[c])
        first.start()
        second.start()
        loads.append((first, second))

    barrier = pltpu.get_barrier_semaphore()
    for s in range(REPS - 1):
        pl.semaphore_signal(barrier, inc=1, device_id=(reps[s], fsdp), device_id_type=MESH)
    for d in range(1, FSDP):
        pl.semaphore_signal(
            barrier, inc=1, device_id=(rep, (fsdp + d) % FSDP), device_id_type=MESH
        )

    local_p = jnp.zeros((RANK, shard.shape[1]), F32)
    for c in range(REPS):
        for load in loads[c]:
            load.wait()
        local_p += lax.dot_general(
            startq[c], shard[c], (((1,), (1,)), ((), ())), preferred_element_type=F32
        )
    p_all[rep] = local_p
    pl.semaphore_wait(barrier, REPS - 1 + FSDP - 1)
    sends = []

    copies = [
        remote(p_all.at[rep], p_all.at[rep], p_send.at[s], p_recv.at[s], reps[s], fsdp)
        for s in range(REPS - 1)
    ]
    for copy in copies:
        copy.wait_recv()
    p_sum = p_all[0] + p_all[1] + p_all[2] + p_all[3]
    padded = jnp.concatenate([p_sum, jnp.zeros((128 - RANK, p_sum.shape[1]), F32)], axis=0)
    g_all[fsdp] = lax.dot_general(
        p_sum, padded, (((1,), (1,)), ((), ())),
        precision=lax.Precision.HIGHEST, preferred_element_type=F32,
    )
    sends += copies
    copies = [
        remote(
            g_all.at[fsdp], g_all.at[fsdp], g_send.at[d - 1], g_recv.at[d - 1],
            rep, (fsdp + d) % FSDP,
        )
        for d in range(1, FSDP)
    ]
    for copy in copies:
        copy.wait_recv()
    sends += copies
    gram = g_all[0]
    for i in range(1, FSDP):
        gram = gram + g_all[i]

    g = [gram[8 * t : 8 * t + 8] for t in range(RANK // 8)]
    p = [p_sum[8 * t : 8 * t + 8] for t in range(RANK // 8)]
    line = lax.broadcasted_iota(jnp.int32, (8, 128), 0)
    pivots = [jnp.ones((8, 128), F32) for _ in g]
    for k in range(RANK):
        t, r = k // 8, k % 8
        row_g, row_p = g[t][r : r + 1], p[t][r : r + 1]
        pivot = row_g[:, k : k + 1]
        pivots[t] = jnp.where(line == r, pivot, pivots[t])
        inverse = 1.0 / pivot
        row_g, row_p = row_g * inverse, row_p * inverse
        for u in range(t, RANK // 8):
            factor = jnp.broadcast_to(g[u][:, k : k + 1], (8, 128))
            if u == t:
                factor = jnp.where(line > r, factor, 0.0)
            g[u] = g[u] - factor * row_g
            p[u] = p[u] - factor * row_p
    p_hat = [p[t] * lax.rsqrt(pivots[t]) for t in range(RANK // 8)]
    p_round = jnp.concatenate(p_hat, axis=0).astype(BF16)
    lower_half = jnp.concatenate(p_hat[:2], axis=0)
    upper_half = jnp.concatenate(p_hat[2:], axis=0)
    is_first = core == 0
    own_first = jnp.concatenate(
        [jnp.where(is_first, lower_half, upper_half), jnp.where(is_first, upper_half, lower_half)],
        axis=0,
    ).astype(BF16)

    quarters = [(z + d) % CHIPS for d in AWAY + (0,)]
    pieces = [(i, s) for i in range(CHIPS) for s in range(REPS - 1)]
    pieces += [(i, REPS - 1) for i in range(CHIPS)]
    core_copies, rep_copies = [], {}

    def to_replica(n):
        i, s = pieces[n]
        core_copies[n].wait_recv()
        summed = own_q[n] + core_in[n].astype(F32)
        if s < REPS - 1:
            rep_out[n] = summed.astype(BF16)
            rep_copies[i, s] = remote(
                rep_out.at[n], rep_in.at[n], rep_send.at[n], rep_recv.at[n], reps[s], fsdp
            )
        else:
            total[i] = summed

    for n, (i, s) in enumerate(pieces):
        columns = pl.ds(pl.multiple_of(quarters[i] * piece, 128), piece)
        terms = jnp.dot(own_first, shard[reps[s], :, columns], preferred_element_type=F32)
        own_q[n] = terms[:HALF]
        core_out[n] = terms[HALF:].astype(BF16)
        core_copies.append(
            remote(
                core_out.at[n], core_in.at[n], core_send.at[n], core_recv.at[n], rep, partner
            )
        )
        if n >= LAG:
            to_replica(n - LAG)
    for n in range(len(pieces) - LAG, len(pieces)):
        to_replica(n)
    sends += core_copies + list(rep_copies.values())

    z_copies = []
    for i in range(CHIPS):
        value = total[i]
        for s in range(REPS - 1):
            rep_copies[i, s].wait_recv()
            value = value + rep_in[pieces.index((i, s))].astype(F32)
        if i < CHIPS - 1:
            z_out[i] = value.astype(BF16)
            z_copies.append(
                remote(
                    z_out.at[i], z_in.at[i], z_send.at[i], z_recv.at[i],
                    rep, quarters[i] * 2 + core,
                )
            )
        else:
            mine = value
    sends += z_copies
    for copy, i in zip(z_copies, range(CHIPS - 1)):
        copy.wait_recv()
        mine = mine + z_in[i].astype(F32)
    final[...] = mine
    gathered[core, z] = mine.astype(BF16)
    ag_copies = [
        remote(
            gathered.at[core, z], gathered.at[core, z], ag_send.at[i], ag_recv.at[i],
            rep, quarters[i] * 2 + core,
        )
        for i in range(CHIPS - 1)
    ]
    relays = [
        remote(
            gathered.at[core, z], gathered.at[core, z], relay_send.at[CHIPS - 1],
            relay_recv.at[CHIPS - 1], rep, partner,
        )
    ]
    fin_copy = remote(final, final_in, fin_send, fin_recv, rep, partner)
    squares = jnp.sum(jnp.sum(mine * mine, axis=0, keepdims=True), axis=1, keepdims=True)
    norms[rep] = jnp.broadcast_to(squares, (8, 128))
    norm_copies = [
        remote(norms.at[rep], norms.at[rep], norm_send.at[s], norm_recv.at[s], reps[s], fsdp)
        for s in range(REPS - 1)
    ]
    nextq_ref[pl.ds(pl.multiple_of(core * HALF, HALF), HALF), :] = mine
    for copy in norm_copies:
        copy.wait_recv()
    all_norms[fsdp] = norms[0] + norms[1] + norms[2] + norms[3]
    all_copies = [
        remote(
            all_norms.at[fsdp], all_norms.at[fsdp], all_send.at[d - 1], all_recv.at[d - 1],
            rep, (fsdp + d) % FSDP,
        )
        for d in range(1, FSDP)
    ]
    sources = [(z + CHIPS - d) % CHIPS for d in AWAY] + [z]
    for i in range(CHIPS - 1):
        ag_copies[i].wait_recv()
        relays.append(
            remote(
                gathered.at[core, sources[i]], gathered.at[core, sources[i]],
                relay_send.at[i], relay_recv.at[i], rep, partner,
            )
        )
    fin_copy.wait_recv()
    nextq_ref[pl.ds(pl.multiple_of((1 - core) * HALF, HALF), HALF), :] = final_in[...]
    sends += ag_copies + relays + [fin_copy] + norm_copies + all_copies
    for copy, q in zip(relays, sources[-1:] + sources[:-1]):
        copy.wait_recv()
        right = jnp.concatenate([gathered[0, q], gathered[1, q]], axis=0)
        products[q] = lax.dot_general(
            p_round, right, (((0,), (0,)), ((), ())), preferred_element_type=F32
        )
    for copy in all_copies:
        copy.wait_recv()
    norm_sq = all_norms[0]
    for i in range(1, FSDP):
        norm_sq = norm_sq + all_norms[i]
    limit = max_rms[0] * math.sqrt(elements)
    scale = jnp.minimum(1.0, limit / jnp.sqrt(norm_sq[:1, :1]))
    for q in range(CHIPS):
        update_ref[:, pl.ds(q * piece, piece)] = (scale * products[q]).astype(BF16)
    for copy in sends:
        copy.wait_send()


def on_block(accumulated, start_q, max_rms):
    rows, width = accumulated.shape[1:]
    block = width // REPS
    piece = block // CHIPS
    dma = pltpu.SemaphoreType.DMA
    update, chip_q = pl.pallas_call(
        round_kernel,
        out_shape=(
            jax.ShapeDtypeStruct((rows, block), BF16),
            jax.ShapeDtypeStruct((RANK, piece), F32),
        ),
        in_specs=[
            pl.BlockSpec(memory_space=pltpu.HBM),
            pl.BlockSpec(memory_space=pltpu.HBM),
            pl.BlockSpec(memory_space=pltpu.SMEM),
        ],
        out_specs=(
            pl.BlockSpec(memory_space=pltpu.VMEM),
            pl.BlockSpec(memory_space=pltpu.VMEM),
        ),
        scratch_shapes=[
            pltpu.VMEM((REPS, rows, block), BF16),
            pltpu.VMEM((REPS, RANK, block), BF16),
            pltpu.VMEM((REPS, RANK, rows), F32),
            pltpu.VMEM((FSDP, RANK, 128), F32),
            pltpu.VMEM((REPS * CHIPS, HALF, piece), F32),
            pltpu.VMEM((REPS * CHIPS, HALF, piece), BF16),
            pltpu.VMEM((REPS * CHIPS, HALF, piece), BF16),
            pltpu.VMEM(((REPS - 1) * CHIPS, HALF, piece), BF16),
            pltpu.VMEM(((REPS - 1) * CHIPS, HALF, piece), BF16),
            pltpu.VMEM((CHIPS, HALF, piece), F32),
            pltpu.VMEM((CHIPS - 1, HALF, piece), BF16),
            pltpu.VMEM((CHIPS - 1, HALF, piece), BF16),
            pltpu.VMEM((2, CHIPS, HALF, piece), BF16),
            pltpu.VMEM((HALF, piece), F32),
            pltpu.VMEM((HALF, piece), F32),
            pltpu.VMEM((REPS, 8, 128), F32),
            pltpu.VMEM((FSDP, 8, 128), F32),
            pltpu.VMEM((CHIPS, rows, piece), F32),
            dma((REPS,)), dma((REPS,)),
            dma((REPS - 1,)), dma((REPS - 1,)),
            dma((FSDP - 1,)), dma((FSDP - 1,)),
            dma((REPS * CHIPS,)), dma((REPS * CHIPS,)),
            dma(((REPS - 1) * CHIPS,)), dma(((REPS - 1) * CHIPS,)),
            dma((CHIPS - 1,)), dma((CHIPS - 1,)),
            dma((CHIPS - 1,)), dma((CHIPS - 1,)),
            dma((CHIPS,)), dma((CHIPS,)),
            dma, dma,
            dma((REPS - 1,)), dma((REPS - 1,)),
            dma((FSDP - 1,)), dma((FSDP - 1,)),
        ],
        compiler_params=pltpu.CompilerParams(
            collective_id=0, has_side_effects=True, vmem_limit_bytes=40 * 1024 * 1024
        ),
    )(accumulated, start_q, max_rms)
    own = piece // 2
    next_q = lax.dynamic_slice_in_dim(chip_q, (lax.axis_index("fsdp") % 2) * own, own, 1)
    return (update, next_q)


def orthonormal(part_rows, gram):
    lower = jnp.linalg.cholesky(gram)
    return lax.linalg.triangular_solve(
        lower, part_rows, left_side=False, lower=True, transpose_a=True
    )


def on_device(accumulated, start_q, max_rms):
    shard = accumulated[0]
    rows = shard.shape[0]
    width = shard.shape[1]
    n_rep = lax.axis_size("rep")
    n_fsdp = lax.axis_size("fsdp")
    total_rows = rows * n_fsdp
    local_p = lax.dot_general(
        shard, start_q, (((1,), (1,)), ((), ())), preferred_element_type=jnp.float32
    )
    p_sum = lax.psum(local_p, "rep")
    gram = lax.psum(jnp.dot(p_sum.T, p_sum, precision=lax.Precision.HIGHEST), "fsdp")
    p_round = orthonormal(p_sum, gram).astype(jnp.bfloat16)
    block_cols = width // n_rep
    own_cols = width // (n_rep * n_fsdp)
    q_full = lax.psum(
        lax.dot_general(
            p_round, shard, (((0,), (0,)), ((), ())), preferred_element_type=jnp.float32
        ),
        ("rep", "fsdp"),
    )
    norm_sq = jnp.sum(q_full * q_full)
    q_block = lax.dynamic_slice_in_dim(
        q_full, lax.axis_index("rep") * block_cols, block_cols, 1
    ).astype(jnp.bfloat16)
    product = jnp.dot(p_round, q_block, preferred_element_type=jnp.float32)
    next_q = lax.dynamic_slice_in_dim(
        q_full, lax.axis_index(("rep", "fsdp")) * own_cols, own_cols, 1
    )
    scale = jnp.minimum(1.0, max_rms[0] * math.sqrt(total_rows * width) / jnp.sqrt(norm_sq))
    update = (scale * product).astype(jnp.bfloat16)
    return (update, next_q)


def solution(mesh):
    fits = mesh.shape["rep"] == REPS and mesh.shape["fsdp"] == FSDP
    return jax.shard_map(
        on_block if fits else on_device,
        mesh=mesh,
        in_specs=(P("rep", "fsdp", None), P(), P()),
        out_specs=(P("fsdp", "rep"), P(None, ("rep", "fsdp"))),
        check_vma=False,
    )
```
